32 devices in a mesh: groups: 2 (over y), expert: 4 (over z), dp: 2 (over x), sub: 2 (over core).
Axes of the slice: x: 2, y: 2, z: 4, core: 2. Of those that a mesh axis runs over, the one named last changes fastest.
Arguments:
- tokens: bfloat16 [8192, 1024], P(('groups', 'expert', 'dp', 'sub')), parts along dimension 0, may hold values from -6 to 6
- upstream: bfloat16 [8192, 1024], P(('groups', 'expert', 'dp', 'sub')), parts along dimension 0, may hold values from -6 to 6
- routes: int32 [8192, 2], P(('groups', 'expert', 'dp', 'sub')), parts along dimension 0, may hold values from 0 to 3, all different within a row; in each aligned block of 256 rows (0 to 255, 256 to 511, ...) at most 192 rows name the same one
- gates: float32 [8192, 2], P(('groups', 'expert', 'dp', 'sub')), parts along dimension 0, may hold values from 0.1 to 1
- w_gate: bfloat16 [4, 1024, 512], P('expert', 'sub'), may hold values from -0.1875 to 0.1875
- w_up: bfloat16 [4, 1024, 512], P('expert', 'sub'), may hold values from -0.1875 to 0.1875
- w_down: bfloat16 [4, 512, 1024], P('expert', None, 'sub'), may hold values from -0.25 to 0.25
Outputs:
- tokens_grad: bfloat16 [8192, 1024], P(('groups', 'expert', 'dp', 'sub')), parts along dimension 0
- grad_gate: float32 [8, 1024, 512], P(('groups', 'expert'), ('dp', 'sub')), parts along dimension 0
- grad_up: float32 [8, 1024, 512], P(('groups', 'expert'), ('dp', 'sub')), parts along dimension 0
- grad_down: float32 [8, 512, 1024], P(('groups', 'expert'), ('dp', 'sub')), parts along dimension 0
The draws below stay inside these ranges and needn't reach their ends.
There are 2 independent parts, one for each index of `groups`. The reference program is written for one: setup_inputs(seed, part) draws one part's arguments, and reference() takes and returns one part's arrays. A program takes and returns all parts, laid end to end along the dimension named above; an argument that names none is the same for every part. Nothing has to cross between parts.
Inputs may be any that keep to these rules, and one draw needn't show every extreme that they name: `routes`: each row names 2 different experts; among the rows of one device no expert is named more than 192 times, and in some device some expert is named exactly 192 times; every expert is named somewhere.
All inputs are finite; a program needn't handle non-finite values.
Results may differ from the reference program's by a relative error of at most 0.0085.
Values may be sent and summed in bfloat16 or wider, within the bound.
A program may use at most 64 MiB of HBM per device.

```python
import math
import jax
import jax.numpy as jnp
import numpy as np
from jax import lax

D = 1024
H = 512
TOP = 2
TOK_DEV = 256
EXPERTS = 4
CAP = 192
TOKENS = 4096
N_DP = 2
N_SUB = 2


def block_levels(own_key, extent, split, smallest, high):
    gain, own = 1.0, jax.random.fold_in(own_key, 6)
    for dim, blocks in split:
        heights = jnp.exp(jax.random.uniform(jax.random.fold_in(own, dim), (blocks,), jnp.float32, smallest / len(split), high / len(split)))
        gain = gain * jnp.repeat(heights, extent[dim] // blocks).reshape([-1 if axis == dim else 1 for axis in range(len(extent))])
    return gain


def shared_out(own_key, own, number, rows, number_of, top, reach, lean):
    sequence = jax.random.permutation(own_key, number_of)
    packed, common = load_shares(number_of, rows * top, reach, lean, True), load_shares(number_of, rows * top, reach, lean, False)
    places = jnp.arange(number_of)

    def named(sizes, offset_by):
        used = int((sizes > 0).sum())
        fixed = max(1, used // 4)
        moved = fixed + (places - fixed + offset_by * (used - fixed)) % max(1, number_of - fixed)
        return jnp.zeros((number_of,), jnp.int32).at[sequence[jnp.where(places < fixed, places, moved)]].set(jnp.asarray(sizes, jnp.int32))

    sizes = jnp.where(number % 4 == 0, named(packed, number // 4), named(common, number - number // 4 - 1))
    mixed = jax.random.permutation(jax.random.fold_in(own, 3), number_of)
    giver, sink = mixed[0:number_of // 2 * 2:2], mixed[1:number_of // 2 * 2:2]
    slack = jnp.minimum(sizes[giver] - 1, reach - sizes[sink]) // 2
    slack = jnp.where((giver == sequence[0]) | (sink == sequence[0]) | (sizes[sink] == 0), 0, jnp.maximum(slack, 0))
    moved = jax.random.randint(jax.random.fold_in(own, 4), (number_of // 2,), 0, 1 << 20) % (slack + 1)
    sizes = sizes.at[giver].add(-moved).at[sink].add(moved)
    labels = jnp.searchsorted(jnp.cumsum(sizes), jnp.arange(rows * top), side="right").astype(jnp.int32)
    listing = labels.reshape(top, rows).T
    listing = listing[jax.random.permutation(jax.random.fold_in(own, 1), rows)]
    offset_by = jax.random.randint(jax.random.fold_in(own, 2), (rows, 1), 0, top)
    return jnp.take_along_axis(listing, (jnp.arange(top)[None, :] + offset_by) % top, axis=1)


def load_shares(amount, total, reach, lean, full):
    loads = [(1 << 20) // math.isqrt(rank ** lean) + 1 for rank in range(1, amount + 1)]
    largest = reach if full else min(reach, max(-(-total // amount), total * loads[0] // sum(loads)))
    least = 1 if total - largest >= amount - 1 else 0
    counts, rest = [largest] + [least] * (amount - 1), total - largest - least * (amount - 1)
    while rest > 0:
        candidates = [i for i in range(1, amount) if counts[i] < largest] or [i for i in range(1, amount) if counts[i] < reach]
        pool, budget = sum([loads[i] for i in candidates]), rest
        for i in candidates:
            extra = min(reach - counts[i], max(1, budget * loads[i] // pool), rest)
            counts[i] = counts[i] + extra
            rest = rest - extra
    return np.array(counts)


def centred(rng, extent, spread, limit, shards=(), kind=jnp.bfloat16):
    array = jax.random.normal(rng, extent, jnp.float32) * spread
    if len(shards) > 0:
        array = block_levels(rng, extent, shards, -0.22, 0.18) * array
    return jnp.clip(array, min=-limit, max=limit).astype(kind)


def setup_inputs(seed: int = 0, part: int = 0) -> dict:
    key_list = jax.random.split(jax.random.key(seed), 8)
    part_splits = jax.random.split(jax.random.fold_in(key_list[7], part), 8)
    tokens = centred(part_splits[0], (TOKENS, D), 1.0, 6.0, ((0, 16),))
    upstream = centred(part_splits[1], (TOKENS, D), 1.0, 6.0, ((0, 16),))
    routes_keys = jax.random.split(jax.random.fold_in(part_splits[2], 1), TOKENS // TOK_DEV)
    routes_turns = jax.random.permutation(jax.random.fold_in(part_splits[2], 3), TOKENS // TOK_DEV)
    routes = jax.vmap(lambda own, number: shared_out(jax.random.fold_in(part_splits[2], 2), own, number, TOK_DEV, EXPERTS, TOP, CAP, 2))(routes_keys, routes_turns).reshape((TOKENS, TOP))
    gates = jnp.clip(0.1 + 0.9 * jax.random.uniform(part_splits[3], (TOKENS, TOP), jnp.float32) ** block_levels(part_splits[3], (TOKENS, TOP), ((0, 16),), -0.2, 0.2), 0.1, 1.0)
    w_gate = centred(key_list[4], (EXPERTS, D, H), D ** -0.5, 0.1875, ((0, 4), (1, 2)))
    w_up = centred(key_list[5], (EXPERTS, D, H), D ** -0.5, 0.1875, ((0, 4), (1, 2)))
    w_down = centred(key_list[6], (EXPERTS, H, D), H ** -0.5, 0.25, ((0, 4), (2, 2)))
    return dict(tokens=tokens, upstream=upstream, routes=routes, gates=gates, w_gate=w_gate, w_up=w_up, w_down=w_down)


def contract(left, right, left_dim, right_dim):
    return lax.dot_general(left, right, (((left_dim,), (right_dim,)), ((), ())), preferred_element_type=jnp.float32)


def expert_backward(gate_pre, up_pre, rows_grad, gate_mat, up_mat, down_mat):
    sigmoid_gate = jax.nn.sigmoid(gate_pre)
    silu_gate = gate_pre * sigmoid_gate
    hidden = (silu_gate * up_pre).astype(jnp.bfloat16)
    hidden_grad = contract(rows_grad, down_mat, 1, 1)
    gate_grad = (hidden_grad * up_pre * sigmoid_gate * (1.0 + gate_pre * (1.0 - sigmoid_gate))).astype(jnp.bfloat16)
    up_grad = (hidden_grad * silu_gate).astype(jnp.bfloat16)
    input_grad = (contract(gate_grad, gate_mat, 1, 1) + contract(up_grad, up_mat, 1, 1)).astype(jnp.bfloat16)
    return hidden, gate_grad, up_grad, input_grad


def group_sum(left, right, source_count, group_count):
    left_blocks = left.astype(jnp.float32).reshape(source_count // group_count, group_count, CAP, left.shape[-1])
    right_blocks = right.astype(jnp.float32).reshape(source_count // group_count, group_count, CAP, right.shape[-1])
    partial_sums = jnp.einsum('agcd,agch->gdh', left_blocks, right_blocks)
    rounded = lax.optimization_barrier(partial_sums.astype(jnp.bfloat16))
    return jnp.sum(rounded.astype(jnp.float32), axis=0)


def reference(tokens, upstream, routes, gates, w_gate, w_up, w_down):
    source_count = TOKENS // TOK_DEV
    group_count = N_DP * N_SUB
    flat_routes = routes.reshape(source_count, TOK_DEV * TOP)
    onehot = (flat_routes[:, :, None] == jnp.arange(EXPERTS, dtype=jnp.int32)[None, None, :]).astype(jnp.int32)
    position = jnp.sum((jnp.cumsum(onehot, axis=1) - 1) * onehot, axis=2).astype(jnp.int32)
    source = jnp.arange(source_count, dtype=jnp.int32)[:, None] * jnp.ones_like(flat_routes)
    pair_ids = jnp.arange(TOKENS * TOP, dtype=jnp.int32).reshape(source_count, TOK_DEV * TOP)
    slot_table = jnp.full((EXPERTS, source_count * CAP), -1, jnp.int32)
    slot_table = slot_table.at[flat_routes.reshape(-1), (source * CAP + position).reshape(-1)].set(pair_ids.reshape(-1))
    gates_flat = gates.reshape(-1)

    def per_expert(summed, inputs):
        slot_ids, gate_mat, up_mat, down_mat = inputs
        usable = slot_ids >= 0
        pair_safe = jnp.where(usable, slot_ids, 0).astype(jnp.int32)
        token_ids = (pair_safe // TOP).astype(jnp.int32)
        rows_in = jnp.where(usable[:, None], tokens[token_ids], jnp.zeros((), jnp.bfloat16))
        weight = jnp.where(usable, gates_flat[pair_safe], jnp.zeros((), gates.dtype))
        rows_grad = (weight[:, None] * upstream[token_ids].astype(jnp.float32)).astype(jnp.bfloat16)
        gate_pre = jnp.dot(rows_in, gate_mat, preferred_element_type=jnp.float32)
        up_pre = jnp.dot(rows_in, up_mat, preferred_element_type=jnp.float32)
        hidden, gate_grad, up_grad, input_grad = expert_backward(gate_pre, up_pre, rows_grad, gate_mat, up_mat, down_mat)
        addend = jnp.where(usable[:, None], input_grad.astype(jnp.float32), jnp.zeros((), jnp.float32))
        summed = summed.at[token_ids].add(addend)
        grad_g = group_sum(rows_in, gate_grad, source_count, group_count)
        grad_u = group_sum(rows_in, up_grad, source_count, group_count)
        grad_d = group_sum(hidden, rows_grad, source_count, group_count)
        return summed, (grad_g, grad_u, grad_d)

    summed, grads = lax.scan(per_expert, jnp.zeros((TOKENS, D), jnp.float32), (slot_table, w_gate, w_up, w_down))
    return summed.astype(jnp.bfloat16), grads[0], grads[1], grads[2]
```

```python
import functools

import jax
import jax.numpy as jnp
from jax import lax
from jax.experimental import pallas as pl
from jax.experimental.pallas import tpu as pltpu
from jax.sharding import PartitionSpec as P

TOP = 2


def contract(left, right, left_dim, right_dim):
    return lax.dot_general(
        left, right, (((left_dim,), (right_dim,)), ((), ())), preferred_element_type=jnp.float32
    )


def expert_backward(gate_pre, up_pre, rows_grad, gate_mat, up_mat, down_mat):
    sigmoid_gate = jax.nn.sigmoid(gate_pre)
    silu_gate = gate_pre * sigmoid_gate
    hidden = (silu_gate * up_pre).astype(jnp.bfloat16)
    hidden_grad = contract(rows_grad, down_mat, 1, 1)
    gate_grad = (
        hidden_grad * up_pre * sigmoid_gate * (1.0 + gate_pre * (1.0 - sigmoid_gate))
    ).astype(jnp.bfloat16)
    up_grad = (hidden_grad * silu_gate).astype(jnp.bfloat16)
    input_grad = (contract(gate_grad, gate_mat, 1, 1) + contract(up_grad, up_mat, 1, 1)).astype(
        jnp.bfloat16
    )
    return (hidden, gate_grad, up_grad, input_grad)


def routed(tokens, upstream, routes, gates, w_gate, w_up, w_down):
    tok_rows, width = tokens.shape
    experts = lax.axis_size("expert") * w_gate.shape[0]
    capacity = min(tok_rows, 3 * tok_rows * TOP // (2 * experts))
    flat_routes = routes.reshape(-1)
    onehot = (flat_routes[:, None] == jnp.arange(experts, dtype=jnp.int32)[None, :]).astype(
        jnp.int32
    )
    position = jnp.sum((jnp.cumsum(onehot, axis=0) - 1) * onehot, axis=1)
    target = flat_routes * capacity + position
    scaled = (
        (gates[:, :, None] * upstream[:, None, :].astype(jnp.float32))
        .astype(jnp.bfloat16)
        .reshape(-1, width)
    )
    repeated = jnp.repeat(tokens, TOP, axis=0)
    empty_rows = jnp.zeros((experts * capacity, width), jnp.bfloat16)
    send_inputs = empty_rows.at[target].set(repeated).reshape(experts, capacity, width)
    send_grads = empty_rows.at[target].set(scaled).reshape(experts, capacity, width)
    whole = (
        lax.all_gather(w_gate, "sub", axis=1, tiled=True),
        lax.all_gather(w_up, "sub", axis=1, tiled=True),
        lax.all_gather(w_down, "sub", axis=2, tiled=True),
    )
    gate_mat, up_mat, down_mat = (whole[0][0], whole[1][0], whole[2][0])
    got_inputs, got_grads = (
        lax.all_to_all(send_inputs, "expert", split_axis=0, concat_axis=0, tiled=True),
        lax.all_to_all(send_grads, "expert", split_axis=0, concat_axis=0, tiled=True),
    )
    rows_in = got_inputs.reshape(-1, width)
    gate_pre = jnp.dot(rows_in, gate_mat, preferred_element_type=jnp.float32)
    up_pre = jnp.dot(rows_in, up_mat, preferred_element_type=jnp.float32)
    rows_grad = got_grads.reshape(-1, width)
    hidden, gate_grad, up_grad, input_grad = expert_backward(
        gate_pre, up_pre, rows_grad, gate_mat, up_mat, down_mat
    )
    returned = lax.all_to_all(
        input_grad.reshape(experts, capacity, width),
        "expert",
        split_axis=0,
        concat_axis=0,
        tiled=True,
    )
    picked = returned.reshape(-1, width)[target].reshape(tok_rows, TOP, width)
    tokens_grad = jnp.sum(picked.astype(jnp.float32), axis=1).astype(jnp.bfloat16)
    part_gate = contract(rows_in, gate_grad, 0, 0)
    part_up = contract(rows_in, up_grad, 0, 0)
    part_down = contract(hidden, rows_grad, 0, 0)
    summed = (
        lax.psum(part_gate.astype(jnp.bfloat16), ("dp", "sub")).astype(jnp.float32),
        lax.psum(part_up.astype(jnp.bfloat16), ("dp", "sub")).astype(jnp.float32),
        lax.psum(part_down.astype(jnp.bfloat16), ("dp", "sub")).astype(jnp.float32),
    )
    pieces = lax.axis_size(("dp", "sub"))
    member = lax.axis_index(("dp", "sub"))
    slices = [
        lax.dynamic_slice_in_dim(
            matrix, member * (matrix.shape[0] // pieces), matrix.shape[0] // pieces, 0
        )
        for matrix in summed
    ]
    return (tokens_grad, slices[0][None], slices[1][None], slices[2][None])

MESH = pl.DeviceIdType.MESH


def fused_kernel(
    n,
    tok_ref,
    ups_ref,
    comb_ref,
    wg_ref,
    wu_ref,
    wd_ref,
    tg_ref,
    gg_ref,
    gu_ref,
    gd_ref,
    x_all,
    u_all,
    c_all,
    w_g,
    w_u,
    w_d,
    back,
    landed,
    acc_g,
    acc_u,
    acc_d,
    sub_gu,
    sub_d,
    got_gu,
    got_d,
    dp_gu,
    dp_d,
    in_gu,
    in_d,
    ag_send,
    ag_recv,
    w_send,
    w_recv,
    ig_send,
    ig_recv,
    rs_send,
    rs_recv,
):
    f32, bf16 = jnp.float32, jnp.bfloat16
    group = lax.axis_index("groups")
    z = lax.axis_index("expert")
    d = lax.axis_index("dp")
    s = lax.axis_index("sub")
    rows_g = acc_g.shape[0] // 4
    rows_d = acc_d.shape[0] // 4
    half = w_d.shape[2]

    def along(position):
        return (group, position, d, s)

    sub_peer = (group, z, d, 1 - s)
    dp_peer = (group, z, 1 - d, s)

    barrier = pltpu.get_barrier_semaphore()
    for step in range(1, n):
        pl.semaphore_signal(
            barrier, inc=1, device_id=along(lax.rem(z + step, n)), device_id_type=MESH
        )
    pl.semaphore_signal(barrier, inc=1, device_id=sub_peer, device_id_type=MESH)
    pl.semaphore_signal(barrier, inc=1, device_id=dp_peer, device_id_type=MESH)
    x_all[z] = tok_ref[...]
    u_all[z] = ups_ref[...]
    c_all[z] = comb_ref[...]
    w_g[s] = wg_ref[...]
    w_u[s] = wu_ref[...]
    w_d[s] = wd_ref[...]
    pl.semaphore_wait(barrier, n + 1)

    def copy(src, dst, send, recv, peer):
        return pltpu.make_async_remote_copy(
            src_ref=src,
            dst_ref=dst,
            send_sem=send,
            recv_sem=recv,
            device_id=peer,
            device_id_type=MESH,
        )

    def block_copies(way, block):
        target = jnp.minimum(z + 1, n - 1) if way == 0 else jnp.maximum(z - 1, 0)
        return [
            copy(
                ref.at[block],
                ref.at[block],
                ag_send.at[way, block, i],
                ag_recv.at[block, i],
                along(target),
            )
            for i, ref in enumerate((c_all, u_all, x_all))
        ]

    can_go = (z < n - 1, z > 0)
    for way in range(2):

        @pl.when(can_go[way])
        def _():
            for each in block_copies(way, z):
                each.start()

    def weight_copies():
        return [
            copy(ref.at[s], ref.at[s], w_send.at[i], w_recv.at[i], sub_peer)
            for i, ref in enumerate((w_g, w_u, w_d))
        ]

    def weight_waits():
        return [
            copy(ref.at[1 - s], ref.at[1 - s], w_send.at[i], w_recv.at[i], sub_peer)
            for i, ref in enumerate((w_g, w_u, w_d))
        ]

    for each in weight_copies():
        each.start()
    acc_g[...] = jnp.zeros_like(acc_g)
    acc_u[...] = jnp.zeros_like(acc_u)
    acc_d[...] = jnp.zeros_like(acc_d)
    for each in weight_waits():
        each.wait_recv()

    def back_copy(block):
        return copy(
            back.at[block], landed.at[z], ig_send.at[block], ig_recv.at[z], along(block)
        )

    def work(block):
        x = x_all[block]
        flipped = jnp.transpose(c_all[block])
        lane = lax.broadcasted_iota(jnp.int32, flipped.shape, 1)
        weight = jnp.sum(jnp.where(lane == z, flipped, 0.0), axis=1, keepdims=True)
        rows_grad = (weight * u_all[block].astype(f32)).astype(bf16)
        x_lo, x_hi = x[:, :half], x[:, half:]
        gate_pre = contract(x_lo, w_g[0], 1, 0) + contract(x_hi, w_g[1], 1, 0)
        up_pre = contract(x_lo, w_u[0], 1, 0) + contract(x_hi, w_u[1], 1, 0)
        hidden_grad = contract(rows_grad[:, :half], w_d[0], 1, 1) + contract(
            rows_grad[:, half:], w_d[1], 1, 1
        )
        sig = jax.nn.sigmoid(gate_pre)
        silu = gate_pre * sig
        hidden = (silu * up_pre).astype(bf16)
        gate_grad = (hidden_grad * up_pre * sig * (1.0 + gate_pre * (1.0 - sig))).astype(bf16)
        up_grad = (hidden_grad * silu).astype(bf16)
        for j in range(2):
            back[block, :, j * half : (j + 1) * half] = (
                contract(gate_grad, w_g[j], 1, 1) + contract(up_grad, w_u[j], 1, 1)
            ).astype(bf16)

        @pl.when(block != z)
        def _():
            back_copy(block).start()

        acc_g[...] += contract(x, gate_grad, 0, 0)
        acc_u[...] += contract(x, up_grad, 0, 0)
        acc_d[...] += contract(hidden, rows_grad, 0, 0)

    def turn(i, carry):
        step, side = i // 2, i % 2

        @pl.when((side == 0) & (step > 0))
        def _():
            for way in range(2):
                block = z - step if way == 0 else z + step
                there = block >= 0 if way == 0 else block < n

                @pl.when(there)
                def _():
                    for each in block_copies(way, block):
                        each.wait_recv()

                @pl.when(there & can_go[way])
                def _():
                    for each in block_copies(way, block):
                        each.start()

        block = z - step + 2 * step * side

        @pl.when((block >= 0) & (block < n))
        def _():
            work(block)

        return carry

    work(z)
    lax.fori_loop(2, 2 * n, turn, 0)

    def piece_g(dd, ss):
        return pl.ds(pl.multiple_of((dd * 2 + ss) * rows_g, rows_g), rows_g)

    def piece_d(dd, ss):
        return pl.ds(pl.multiple_of((dd * 2 + ss) * rows_d, rows_d), rows_d)

    for dd in range(2):
        sub_gu[0, dd] = acc_g[piece_g(dd, 1 - s), :].astype(bf16)
        sub_gu[1, dd] = acc_u[piece_g(dd, 1 - s), :].astype(bf16)
        sub_d[dd] = acc_d[piece_d(dd, 1 - s), :].astype(bf16)
    to_sub = [
        copy(sub_gu, got_gu, rs_send.at[0], rs_recv.at[0], sub_peer),
        copy(sub_d, got_d, rs_send.at[1], rs_recv.at[1], sub_peer),
    ]
    for each in to_sub:
        each.start()
    for each in to_sub:
        each.wait_recv()

    def pair(acc, rows, got):
        return acc[rows, :].astype(bf16).astype(f32) + got.astype(f32)

    other = 1 - d
    dp_gu[0] = pair(acc_g, piece_g(other, s), got_gu[0, other]).astype(bf16)
    dp_gu[1] = pair(acc_u, piece_g(other, s), got_gu[1, other]).astype(bf16)
    dp_d[...] = pair(acc_d, piece_d(other, s), got_d[other]).astype(bf16)
    to_dp = [
        copy(dp_gu, in_gu, rs_send.at[2], rs_recv.at[2], dp_peer),
        copy(dp_d, in_d, rs_send.at[3], rs_recv.at[3], dp_peer),
    ]
    for each in to_dp:
        each.start()
    gg_ref[...] = pair(acc_g, piece_g(d, s), got_gu[0, d])
    gu_ref[...] = pair(acc_u, piece_g(d, s), got_gu[1, d])
    gd_ref[...] = pair(acc_d, piece_d(d, s), got_d[d])

    landed[z] = back[z]
    for source in range(n):

        @pl.when(z != source)
        def _():
            copy(
                back.at[source],
                landed.at[source],
                ig_send.at[source],
                ig_recv.at[source],
                along(source),
            ).wait_recv()

    total = landed[0].astype(f32)
    for source in range(1, n):
        total = total + landed[source].astype(f32)
    tg_ref[...] = total.astype(bf16)
    for each in to_dp:
        each.wait_recv()
    gg_ref[...] += in_gu[0].astype(f32)
    gu_ref[...] += in_gu[1].astype(f32)
    gd_ref[...] += in_d[...].astype(f32)

    for each in to_sub + to_dp + weight_copies():
        each.wait_send()
    for block in range(n):

        @pl.when(z != block)
        def _():
            back_copy(block).wait_send()

        for way in range(2):
            mine = z >= block if way == 0 else z <= block

            @pl.when(mine & can_go[way])
            def _():
                for each in block_copies(way, block):
                    each.wait_send()


def fused(tokens, upstream, routes, gates, w_gate, w_up, w_down):
    f32, bf16 = jnp.float32, jnp.bfloat16
    rows, width = tokens.shape
    n = lax.axis_size("expert")
    depth, hid = w_gate.shape[1:]
    lines = -(-n // 8) * 8
    names = jnp.arange(lines, dtype=jnp.int32)[:, None]
    comb = sum(
        jnp.where(routes[:, k][None, :] == names, gates[:, k][None, :], 0.0) for k in range(TOP)
    )
    dma = pltpu.SemaphoreType.DMA
    quarter_g, quarter_d = width // 4, hid // 4
    outs = pl.pallas_call(
        functools.partial(fused_kernel, n),
        out_shape=(
            jax.ShapeDtypeStruct((rows, width), bf16),
            jax.ShapeDtypeStruct((quarter_g, hid), f32),
            jax.ShapeDtypeStruct((quarter_g, hid), f32),
            jax.ShapeDtypeStruct((quarter_d, width), f32),
        ),
        in_specs=[pl.BlockSpec(memory_space=pltpu.VMEM)] * 6,
        out_specs=[pl.BlockSpec(memory_space=pltpu.VMEM)] * 4,
        scratch_shapes=[
            pltpu.VMEM((n, rows, width), bf16),
            pltpu.VMEM((n, rows, width), bf16),
            pltpu.VMEM((n, lines, rows), f32),
            pltpu.VMEM((2, depth, hid), bf16),
            pltpu.VMEM((2, depth, hid), bf16),
            pltpu.VMEM((2, hid, w_down.shape[2]), bf16),
            pltpu.VMEM((n, rows, width), bf16),
            pltpu.VMEM((n, rows, width), bf16),
            pltpu.VMEM((width, hid), f32),
            pltpu.VMEM((width, hid), f32),
            pltpu.VMEM((hid, width), f32),
            pltpu.VMEM((2, 2, quarter_g, hid), bf16),
            pltpu.VMEM((2, quarter_d, width), bf16),
            pltpu.VMEM((2, 2, quarter_g, hid), bf16),
            pltpu.VMEM((2, quarter_d, width), bf16),
            pltpu.VMEM((2, quarter_g, hid), bf16),
            pltpu.VMEM((quarter_d, width), bf16),
            pltpu.VMEM((2, quarter_g, hid), bf16),
            pltpu.VMEM((quarter_d, width), bf16),
            dma((2, n, 3)),
            dma((n, 3)),
            dma((3,)),
            dma((3,)),
            dma((n,)),
            dma((n,)),
            dma((4,)),
            dma((4,)),
        ],
        compiler_params=pltpu.CompilerParams(
            collective_id=0, has_side_effects=True, vmem_limit_bytes=56 * 1024 * 1024
        ),
    )(tokens, upstream, comb, w_gate[0], w_up[0], w_down[0])
    return (outs[0], outs[1][None], outs[2][None], outs[3][None])


def per_device(*args):
    small = lax.axis_size("expert") <= 2 * TOP and args[4].shape[0] == 1
    if small and lax.axis_size("dp") == 2 and lax.axis_size("sub") == 2:
        return fused(*args)
    return routed(*args)


def solution(mesh):
    in_specs = (
        P(("groups", "expert", "dp", "sub"), None),
        P(("groups", "expert", "dp", "sub"), None),
        P(("groups", "expert", "dp", "sub"), None),
        P(("groups", "expert", "dp", "sub"), None),
        P("expert", "sub", None),
        P("expert", "sub", None),
        P("expert", None, "sub"),
    )
    out_specs = (
        P(("groups", "expert", "dp", "sub"), None),
        P(("groups", "expert"), ("dp", "sub"), None),
        P(("groups", "expert"), ("dp", "sub"), None),
        P(("groups", "expert"), ("dp", "sub"), None),
    )
    return jax.shard_map(
        per_device, mesh=mesh, in_specs=in_specs, out_specs=out_specs, check_vma=False
    )
```

```python
import functools

import jax
import jax.numpy as jnp
from jax import lax
from jax.experimental import pallas as pl
from jax.experimental.pallas import tpu as pltpu
from jax.sharding import PartitionSpec as P

TOP = 2


def contract(left, right, left_dim, right_dim):
    return lax.dot_general(
        left, right, (((left_dim,), (right_dim,)), ((), ())), preferred_element_type=jnp.float32
    )


def expert_backward(gate_pre, up_pre, rows_grad, gate_mat, up_mat, down_mat):
    sigmoid_gate = jax.nn.sigmoid(gate_pre)
    silu_gate = gate_pre * sigmoid_gate
    hidden = (silu_gate * up_pre).astype(jnp.bfloat16)
    hidden_grad = contract(rows_grad, down_mat, 1, 1)
    gate_grad = (
        hidden_grad * up_pre * sigmoid_gate * (1.0 + gate_pre * (1.0 - sigmoid_gate))
    ).astype(jnp.bfloat16)
    up_grad = (hidden_grad * silu_gate).astype(jnp.bfloat16)
    input_grad = (contract(gate_grad, gate_mat, 1, 1) + contract(up_grad, up_mat, 1, 1)).astype(
        jnp.bfloat16
    )
    return (hidden, gate_grad, up_grad, input_grad)


def routed(tokens, upstream, routes, gates, w_gate, w_up, w_down):
    tok_rows, width = tokens.shape
    experts = lax.axis_size("expert") * w_gate.shape[0]
    capacity = min(tok_rows, 3 * tok_rows * TOP // (2 * experts))
    flat_routes = routes.reshape(-1)
    onehot = (flat_routes[:, None] == jnp.arange(experts, dtype=jnp.int32)[None, :]).astype(
        jnp.int32
    )
    position = jnp.sum((jnp.cumsum(onehot, axis=0) - 1) * onehot, axis=1)
    target = flat_routes * capacity + position
    scaled = (
        (gates[:, :, None] * upstream[:, None, :].astype(jnp.float32))
        .astype(jnp.bfloat16)
        .reshape(-1, width)
    )
    repeated = jnp.repeat(tokens, TOP, axis=0)
    empty_rows = jnp.zeros((experts * capacity, width), jnp.bfloat16)
    send_inputs = empty_rows.at[target].set(repeated).reshape(experts, capacity, width)
    send_grads = empty_rows.at[target].set(scaled).reshape(experts, capacity, width)
    whole = (
        lax.all_gather(w_gate, "sub", axis=1, tiled=True),
        lax.all_gather(w_up, "sub", axis=1, tiled=True),
        lax.all_gather(w_down, "sub", axis=2, tiled=True),
    )
    gate_mat, up_mat, down_mat = (whole[0][0], whole[1][0], whole[2][0])
    got_inputs, got_grads = (
        lax.all_to_all(send_inputs, "expert", split_axis=0, concat_axis=0, tiled=True),
        lax.all_to_all(send_grads, "expert", split_axis=0, concat_axis=0, tiled=True),
    )
    rows_in = got_inputs.reshape(-1, width)
    gate_pre = jnp.dot(rows_in, gate_mat, preferred_element_type=jnp.float32)
    up_pre = jnp.dot(rows_in, up_mat, preferred_element_type=jnp.float32)
    rows_grad = got_grads.reshape(-1, width)
    hidden, gate_grad, up_grad, input_grad = expert_backward(
        gate_pre, up_pre, rows_grad, gate_mat, up_mat, down_mat
    )
    returned = lax.all_to_all(
        input_grad.reshape(experts, capacity, width),
        "expert",
        split_axis=0,
        concat_axis=0,
        tiled=True,
    )
    picked = returned.reshape(-1, width)[target].reshape(tok_rows, TOP, width)
    tokens_grad = jnp.sum(picked.astype(jnp.float32), axis=1).astype(jnp.bfloat16)
    part_gate = contract(rows_in, gate_grad, 0, 0)
    part_up = contract(rows_in, up_grad, 0, 0)
    part_down = contract(hidden, rows_grad, 0, 0)
    summed = (
        lax.psum(part_gate.astype(jnp.bfloat16), ("dp", "sub")).astype(jnp.float32),
        lax.psum(part_up.astype(jnp.bfloat16), ("dp", "sub")).astype(jnp.float32),
        lax.psum(part_down.astype(jnp.bfloat16), ("dp", "sub")).astype(jnp.float32),
    )
    pieces = lax.axis_size(("dp", "sub"))
    member = lax.axis_index(("dp", "sub"))
    slices = [
        lax.dynamic_slice_in_dim(
            matrix, member * (matrix.shape[0] // pieces), matrix.shape[0] // pieces, 0
        )
        for matrix in summed
    ]
    return (tokens_grad, slices[0][None], slices[1][None], slices[2][None])

MESH = pl.DeviceIdType.MESH
CHUNKS = 4


def fused_kernel(
    n,
    tok_ref,
    ups_ref,
    comb_ref,
    wg_ref,
    wu_ref,
    wd_ref,
    tg_ref,
    gg_ref,
    gu_ref,
    gd_ref,
    x_all,
    u_all,
    c_all,
    w_g,
    w_u,
    w_d,
    back,
    landed,
    acc_g,
    acc_u,
    acc_d,
    sub_gu,
    sub_d,
    got_gu,
    got_d,
    dp_gu,
    dp_d,
    in_gu,
    in_d,
    ag_send,
    ag_recv,
    w_send,
    w_recv,
    ig_send,
    ig_recv,
    rs_send,
    rs_recv,
):
    f32, bf16 = jnp.float32, jnp.bfloat16
    group = lax.axis_index("groups")
    z = lax.axis_index("expert")
    d = lax.axis_index("dp")
    s = lax.axis_index("sub")
    rows_g = acc_g.shape[0] // 4
    rows_d = acc_d.shape[0] // 4
    half = w_d.shape[2]

    def along(position):
        return (group, position, d, s)

    sub_peer = (group, z, d, 1 - s)
    dp_peer = (group, z, 1 - d, s)

    barrier = pltpu.get_barrier_semaphore()
    for step in range(1, n):
        pl.semaphore_signal(
            barrier, inc=1, device_id=along(lax.rem(z + step, n)), device_id_type=MESH
        )
    pl.semaphore_signal(barrier, inc=1, device_id=sub_peer, device_id_type=MESH)
    pl.semaphore_signal(barrier, inc=1, device_id=dp_peer, device_id_type=MESH)
    x_all[z] = tok_ref[...]
    u_all[z] = ups_ref[...]
    c_all[z] = comb_ref[...]
    w_g[s] = wg_ref[...]
    w_u[s] = wu_ref[...]
    w_d[s] = wd_ref[...]
    pl.semaphore_wait(barrier, n + 1)

    def copy(src, dst, send, recv, peer):
        return pltpu.make_async_remote_copy(
            src_ref=src,
            dst_ref=dst,
            send_sem=send,
            recv_sem=recv,
            device_id=peer,
            device_id_type=MESH,
        )

    def block_copies(way, block):
        target = jnp.minimum(z + 1, n - 1) if way == 0 else jnp.maximum(z - 1, 0)
        return [
            copy(
                ref.at[block],
                ref.at[block],
                ag_send.at[way, block, i],
                ag_recv.at[block, i],
                along(target),
            )
            for i, ref in enumerate((c_all, u_all, x_all))
        ]

    can_go = (z < n - 1, z > 0)
    for way in range(2):

        @pl.when(can_go[way])
        def _():
            for each in block_copies(way, z):
                each.start()

    def weight_copies():
        return [
            copy(ref.at[s], ref.at[s], w_send.at[i], w_recv.at[i], sub_peer)
            for i, ref in enumerate((w_g, w_u, w_d))
        ]

    def weight_waits():
        return [
            copy(ref.at[1 - s], ref.at[1 - s], w_send.at[i], w_recv.at[i], sub_peer)
            for i, ref in enumerate((w_g, w_u, w_d))
        ]

    for each in weight_copies():
        each.start()
    acc_g[...] = jnp.zeros_like(acc_g)
    acc_u[...] = jnp.zeros_like(acc_u)
    acc_d[...] = jnp.zeros_like(acc_d)
    for each in weight_waits():
        each.wait_recv()

    tall = back.shape[1] // CHUNKS

    def back_copy(way, block, chunk):
        rows = pl.ds(chunk * tall, tall)
        target = jnp.minimum(z + 1, n - 1) if way == 0 else jnp.maximum(z - 1, 0)
        return copy(
            back.at[block, rows],
            landed.at[way, block, rows],
            ig_send.at[block, chunk],
            ig_recv.at[way, block, chunk],
            along(target),
        )

    def work(block):
        x = x_all[block]
        flipped = jnp.transpose(c_all[block])
        lane = lax.broadcasted_iota(jnp.int32, flipped.shape, 1)
        weight = jnp.sum(jnp.where(lane == z, flipped, 0.0), axis=1, keepdims=True)
        rows_grad = (weight * u_all[block].astype(f32)).astype(bf16)
        x_lo, x_hi = x[:, :half], x[:, half:]
        gate_pre = contract(x_lo, w_g[0], 1, 0) + contract(x_hi, w_g[1], 1, 0)
        up_pre = contract(x_lo, w_u[0], 1, 0) + contract(x_hi, w_u[1], 1, 0)
        hidden_grad = contract(rows_grad[:, :half], w_d[0], 1, 1) + contract(
            rows_grad[:, half:], w_d[1], 1, 1
        )
        sig = jax.nn.sigmoid(gate_pre)
        silu = gate_pre * sig
        hidden = (silu * up_pre).astype(bf16)
        gate_grad = (hidden_grad * up_pre * sig * (1.0 + gate_pre * (1.0 - sig))).astype(bf16)
        up_grad = (hidden_grad * silu).astype(bf16)
        for j in range(2):
            back[block, :, j * half : (j + 1) * half] = (
                contract(gate_grad, w_g[j], 1, 1) + contract(up_grad, w_u[j], 1, 1)
            ).astype(bf16)

        for way in range(2):
            first = (z == 0) & (block > z) if way == 0 else (z == n - 1) & (block < z)

            @pl.when(first)
            def _():
                for chunk in range(CHUNKS):
                    back_copy(way, block, chunk).start()

        acc_g[...] += contract(x, gate_grad, 0, 0)
        acc_u[...] += contract(x, up_grad, 0, 0)
        acc_d[...] += contract(hidden, rows_grad, 0, 0)

    def turn(i, carry):
        step, side = i // 2, i % 2

        @pl.when((side == 0) & (step > 0))
        def _():
            for way in range(2):
                block = z - step if way == 0 else z + step
                there = block >= 0 if way == 0 else block < n

                @pl.when(there)
                def _():
                    for each in block_copies(way, block):
                        each.wait_recv()

                @pl.when(there & can_go[way])
                def _():
                    for each in block_copies(way, block):
                        each.start()

        block = z - step + 2 * step * side

        @pl.when((block >= 0) & (block < n))
        def _():
            work(block)

        return carry

    work(z)
    lax.fori_loop(2, 2 * n, turn, 0)

    def piece_g(dd, ss):
        return pl.ds(pl.multiple_of((dd * 2 + ss) * rows_g, rows_g), rows_g)

    def piece_d(dd, ss):
        return pl.ds(pl.multiple_of((dd * 2 + ss) * rows_d, rows_d), rows_d)

    for dd in range(2):
        sub_gu[0, dd] = acc_g[piece_g(dd, 1 - s), :].astype(bf16)
        sub_gu[1, dd] = acc_u[piece_g(dd, 1 - s), :].astype(bf16)
        sub_d[dd] = acc_d[piece_d(dd, 1 - s), :].astype(bf16)
    to_sub = [
        copy(sub_gu, got_gu, rs_send.at[0], rs_recv.at[0], sub_peer),
        copy(sub_d, got_d, rs_send.at[1], rs_recv.at[1], sub_peer),
    ]
    for each in to_sub:
        each.start()
    for each in to_sub:
        each.wait_recv()

    def pair(acc, rows, got):
        return acc[rows, :].astype(bf16).astype(f32) + got.astype(f32)

    other = 1 - d
    dp_gu[0] = pair(acc_g, piece_g(other, s), got_gu[0, other]).astype(bf16)
    dp_gu[1] = pair(acc_u, piece_g(other, s), got_gu[1, other]).astype(bf16)
    dp_d[...] = pair(acc_d, piece_d(other, s), got_d[other]).astype(bf16)
    to_dp = [
        copy(dp_gu, in_gu, rs_send.at[2], rs_recv.at[2], dp_peer),
        copy(dp_d, in_d, rs_send.at[3], rs_recv.at[3], dp_peer),
    ]
    for each in to_dp:
        each.start()
    gg_ref[...] = pair(acc_g, piece_g(d, s), got_gu[0, d])
    gu_ref[...] = pair(acc_u, piece_g(d, s), got_gu[1, d])
    gd_ref[...] = pair(acc_d, piece_d(d, s), got_d[d])

    for key in range(1, n):
        for chunk in range(CHUNKS):
            rows = pl.ds(chunk * tall, tall)
            for way in range(2):
                block = key if way == 0 else n - 1 - key
                relay = (z > 0) & (z < block) if way == 0 else (z < n - 1) & (z > block)

                @pl.when(relay)
                def _():
                    hop = back_copy(way, block, chunk)
                    hop.wait_recv()
                    back[block, rows] = (
                        back[block, rows].astype(f32) + landed[way, block, rows].astype(f32)
                    ).astype(bf16)
                    hop.start()

    for chunk in range(CHUNKS):
        rows = pl.ds(chunk * tall, tall)
        for way in range(2):

            @pl.when(z > 0 if way == 0 else z < n - 1)
            def _():
                back_copy(way, z, chunk).wait_recv()
                back[z, rows] = (
                    back[z, rows].astype(f32) + landed[way, z, rows].astype(f32)
                ).astype(bf16)

        tg_ref[rows, :] = back[z, rows]
    for each in to_dp:
        each.wait_recv()
    gg_ref[...] += in_gu[0].astype(f32)
    gu_ref[...] += in_gu[1].astype(f32)
    gd_ref[...] += in_d[...].astype(f32)

    for each in to_sub + to_dp + weight_copies():
        each.wait_send()
    for block in range(n):

        for way in range(2):

            @pl.when(z < block if way == 0 else z > block)
            def _():
                for chunk in range(CHUNKS):
                    back_copy(way, block, chunk).wait_send()

        for way in range(2):
            mine = z >= block if way == 0 else z <= block

            @pl.when(mine & can_go[way])
            def _():
                for each in block_copies(way, block):
                    each.wait_send()


def fused(tokens, upstream, routes, gates, w_gate, w_up, w_down):
    f32, bf16 = jnp.float32, jnp.bfloat16
    rows, width = tokens.shape
    n = lax.axis_size("expert")
    depth, hid = w_gate.shape[1:]
    lines = -(-n // 8) * 8
    names = jnp.arange(lines, dtype=jnp.int32)[:, None]
    comb = sum(
        jnp.where(routes[:, k][None, :] == names, gates[:, k][None, :], 0.0) for k in range(TOP)
    )
    dma = pltpu.SemaphoreType.DMA
    quarter_g, quarter_d = width // 4, hid // 4
    outs = pl.pallas_call(
        functools.partial(fused_kernel, n),
        out_shape=(
            jax.ShapeDtypeStruct((rows, width), bf16),
            jax.ShapeDtypeStruct((quarter_g, hid), f32),
            jax.ShapeDtypeStruct((quarter_g, hid), f32),
            jax.ShapeDtypeStruct((quarter_d, width), f32),
        ),
        in_specs=[pl.BlockSpec(memory_space=pltpu.VMEM)] * 6,
        out_specs=[pl.BlockSpec(memory_space=pltpu.VMEM)] * 4,
        scratch_shapes=[
            pltpu.VMEM((n, rows, width), bf16),
            pltpu.VMEM((n, rows, width), bf16),
            pltpu.VMEM((n, lines, rows), f32),
            pltpu.VMEM((2, depth, hid), bf16),
            pltpu.VMEM((2, depth, hid), bf16),
            pltpu.VMEM((2, hid, w_down.shape[2]), bf16),
            pltpu.VMEM((n, rows, width), bf16),
            pltpu.VMEM((2, n, rows, width), bf16),
            pltpu.VMEM((width, hid), f32),
            pltpu.VMEM((width, hid), f32),
            pltpu.VMEM((hid, width), f32),
            pltpu.VMEM((2, 2, quarter_g, hid), bf16),
            pltpu.VMEM((2, quarter_d, width), bf16),
            pltpu.VMEM((2, 2, quarter_g, hid), bf16),
            pltpu.VMEM((2, quarter_d, width), bf16),
            pltpu.VMEM((2, quarter_g, hid), bf16),
            pltpu.VMEM((quarter_d, width), bf16),
            pltpu.VMEM((2, quarter_g, hid), bf16),
            pltpu.VMEM((quarter_d, width), bf16),
            dma((2, n, 3)),
            dma((n, 3)),
            dma((3,)),
            dma((3,)),
            dma((n, CHUNKS)),
            dma((2, n, CHUNKS)),
            dma((4,)),
            dma((4,)),
        ],
        compiler_params=pltpu.CompilerParams(
            collective_id=0, has_side_effects=True, vmem_limit_bytes=56 * 1024 * 1024
        ),
    )(tokens, upstream, comb, w_gate[0], w_up[0], w_down[0])
    return (outs[0], outs[1][None], outs[2][None], outs[3][None])


def per_device(*args):
    small = lax.axis_size("expert") <= 2 * TOP and args[4].shape[0] == 1
    if small and lax.axis_size("dp") == 2 and lax.axis_size("sub") == 2:
        return fused(*args)
    return routed(*args)


def solution(mesh):
    in_specs = (
        P(("groups", "expert", "dp", "sub"), None),
        P(("groups", "expert", "dp", "sub"), None),
        P(("groups", "expert", "dp", "sub"), None),
        P(("groups", "expert", "dp", "sub"), None),
        P("expert", "sub", None),
        P("expert", "sub", None),
        P("expert", None, "sub"),
    )
    out_specs = (
        P(("groups", "expert", "dp", "sub"), None),
        P(("groups", "expert"), ("dp", "sub"), None),
        P(("groups", "expert"), ("dp", "sub"), None),
        P(("groups", "expert"), ("dp", "sub"), None),
    )
    return jax.shard_map(
        per_device, mesh=mesh, in_specs=in_specs, out_specs=out_specs, check_vma=False
    )
```

```python
import functools

import jax
import jax.numpy as jnp
from jax import lax
from jax.experimental import pallas as pl
from jax.experimental.pallas import tpu as pltpu
from jax.sharding import PartitionSpec as P

TOP = 2


def contract(left, right, left_dim, right_dim):
    return lax.dot_general(
        left, right, (((left_dim,), (right_dim,)), ((), ())), preferred_element_type=jnp.float32
    )


def expert_backward(gate_pre, up_pre, rows_grad, gate_mat, up_mat, down_mat):
    sigmoid_gate = jax.nn.sigmoid(gate_pre)
    silu_gate = gate_pre * sigmoid_gate
    hidden = (silu_gate * up_pre).astype(jnp.bfloat16)
    hidden_grad = contract(rows_grad, down_mat, 1, 1)
    gate_grad = (
        hidden_grad * up_pre * sigmoid_gate * (1.0 + gate_pre * (1.0 - sigmoid_gate))
    ).astype(jnp.bfloat16)
    up_grad = (hidden_grad * silu_gate).astype(jnp.bfloat16)
    input_grad = (contract(gate_grad, gate_mat, 1, 1) + contract(up_grad, up_mat, 1, 1)).astype(
        jnp.bfloat16
    )
    return (hidden, gate_grad, up_grad, input_grad)


def routed(tokens, upstream, routes, gates, w_gate, w_up, w_down):
    tok_rows, width = tokens.shape
    experts = lax.axis_size("expert") * w_gate.shape[0]
    capacity = min(tok_rows, 3 * tok_rows * TOP // (2 * experts))
    flat_routes = routes.reshape(-1)
    onehot = (flat_routes[:, None] == jnp.arange(experts, dtype=jnp.int32)[None, :]).astype(
        jnp.int32
    )
    position = jnp.sum((jnp.cumsum(onehot, axis=0) - 1) * onehot, axis=1)
    target = flat_routes * capacity + position
    scaled = (
        (gates[:, :, None] * upstream[:, None, :].astype(jnp.float32))
        .astype(jnp.bfloat16)
        .reshape(-1, width)
    )
    repeated = jnp.repeat(tokens, TOP, axis=0)
    empty_rows = jnp.zeros((experts * capacity, width), jnp.bfloat16)
    send_inputs = empty_rows.at[target].set(repeated).reshape(experts, capacity, width)
    send_grads = empty_rows.at[target].set(scaled).reshape(experts, capacity, width)
    whole = (
        lax.all_gather(w_gate, "sub", axis=1, tiled=True),
        lax.all_gather(w_up, "sub", axis=1, tiled=True),
        lax.all_gather(w_down, "sub", axis=2, tiled=True),
    )
    gate_mat, up_mat, down_mat = (whole[0][0], whole[1][0], whole[2][0])
    got_inputs, got_grads = (
        lax.all_to_all(send_inputs, "expert", split_axis=0, concat_axis=0, tiled=True),
        lax.all_to_all(send_grads, "expert", split_axis=0, concat_axis=0, tiled=True),
    )
    rows_in = got_inputs.reshape(-1, width)
    gate_pre = jnp.dot(rows_in, gate_mat, preferred_element_type=jnp.float32)
    up_pre = jnp.dot(rows_in, up_mat, preferred_element_type=jnp.float32)
    rows_grad = got_grads.reshape(-1, width)
    hidden, gate_grad, up_grad, input_grad = expert_backward(
        gate_pre, up_pre, rows_grad, gate_mat, up_mat, down_mat
    )
    returned = lax.all_to_all(
        input_grad.reshape(experts, capacity, width),
        "expert",
        split_axis=0,
        concat_axis=0,
        tiled=True,
    )
    picked = returned.reshape(-1, width)[target].reshape(tok_rows, TOP, width)
    tokens_grad = jnp.sum(picked.astype(jnp.float32), axis=1).astype(jnp.bfloat16)
    part_gate = contract(rows_in, gate_grad, 0, 0)
    part_up = contract(rows_in, up_grad, 0, 0)
    part_down = contract(hidden, rows_grad, 0, 0)
    summed = (
        lax.psum(part_gate.astype(jnp.bfloat16), ("dp", "sub")).astype(jnp.float32),
        lax.psum(part_up.astype(jnp.bfloat16), ("dp", "sub")).astype(jnp.float32),
        lax.psum(part_down.astype(jnp.bfloat16), ("dp", "sub")).astype(jnp.float32),
    )
    pieces = lax.axis_size(("dp", "sub"))
    member = lax.axis_index(("dp", "sub"))
    slices = [
        lax.dynamic_slice_in_dim(
            matrix, member * (matrix.shape[0] // pieces), matrix.shape[0] // pieces, 0
        )
        for matrix in summed
    ]
    return (tokens_grad, slices[0][None], slices[1][None], slices[2][None])

MESH = pl.DeviceIdType.MESH
CHUNKS = 4
FLIGHT = 4


def fused_kernel(
    n,
    tok_ref,
    ups_ref,
    comb_ref,
    wg_ref,
    wu_ref,
    wd_ref,
    tg_ref,
    gg_ref,
    gu_ref,
    gd_ref,
    x_all,
    u_all,
    c_all,
    w_g,
    w_u,
    w_d,
    back,
    landed,
    acc_g,
    acc_u,
    acc_d,
    sub_gu,
    sub_d,
    got_gu,
    got_d,
    dp_gu,
    dp_d,
    in_gu,
    in_d,
    ag_send,
    ag_recv,
    w_send,
    w_recv,
    ig_send,
    ig_recv,
    rs_send,
    rs_recv,
):
    f32, bf16 = jnp.float32, jnp.bfloat16
    group = lax.axis_index("groups")
    z = lax.axis_index("expert")
    d = lax.axis_index("dp")
    s = lax.axis_index("sub")
    rows_g = acc_g.shape[0] // 4
    rows_d = acc_d.shape[0] // 4
    half = w_d.shape[2]

    def along(position):
        return (group, position, d, s)

    sub_peer = (group, z, d, 1 - s)
    dp_peer = (group, z, 1 - d, s)

    barrier = pltpu.get_barrier_semaphore()
    for step in range(1, n):
        pl.semaphore_signal(
            barrier, inc=1, device_id=along(lax.rem(z + step, n)), device_id_type=MESH
        )
    pl.semaphore_signal(barrier, inc=1, device_id=sub_peer, device_id_type=MESH)
    pl.semaphore_signal(barrier, inc=1, device_id=dp_peer, device_id_type=MESH)
    x_all[z] = tok_ref[...]
    u_all[z] = ups_ref[...]
    c_all[z] = comb_ref[...]
    w_g[s] = wg_ref[...]
    w_u[s] = wu_ref[...]
    w_d[s] = wd_ref[...]
    pl.semaphore_wait(barrier, n + 1)

    def copy(src, dst, send, recv, peer):
        return pltpu.make_async_remote_copy(
            src_ref=src,
            dst_ref=dst,
            send_sem=send,
            recv_sem=recv,
            device_id=peer,
            device_id_type=MESH,
        )

    def block_copies(way, block):
        target = jnp.minimum(z + 1, n - 1) if way == 0 else jnp.maximum(z - 1, 0)
        return [
            copy(
                ref.at[block],
                ref.at[block],
                ag_send.at[way, block, i],
                ag_recv.at[block, i],
                along(target),
            )
            for i, ref in enumerate((c_all, u_all, x_all))
        ]

    can_go = (z < n - 1, z > 0)
    for way in range(2):

        @pl.when(can_go[way])
        def _():
            for each in block_copies(way, z):
                each.start()

    def weight_copies():
        return [
            copy(ref.at[s], ref.at[s], w_send.at[i], w_recv.at[i], sub_peer)
            for i, ref in enumerate((w_g, w_u, w_d))
        ]

    def weight_waits():
        return [
            copy(ref.at[1 - s], ref.at[1 - s], w_send.at[i], w_recv.at[i], sub_peer)
            for i, ref in enumerate((w_g, w_u, w_d))
        ]

    for each in weight_copies():
        each.start()
    acc_g[...] = jnp.zeros_like(acc_g)
    acc_u[...] = jnp.zeros_like(acc_u)
    acc_d[...] = jnp.zeros_like(acc_d)
    for each in weight_waits():
        each.wait_recv()

    tall = back.shape[1] // CHUNKS

    def chunk_rows(chunk):
        return pl.ds(pl.multiple_of(chunk * tall, tall), tall)

    def back_copy(way, block, chunk):
        rows = chunk_rows(chunk)
        target = jnp.minimum(z + 1, n - 1) if way == 0 else jnp.maximum(z - 1, 0)
        return copy(
            back.at[block, rows],
            landed.at[way, block, rows],
            ig_send.at[block, chunk],
            ig_recv.at[way, block, chunk],
            along(target),
        )

    def work(block):
        x = x_all[block]
        flipped = jnp.transpose(c_all[block])
        lane = lax.broadcasted_iota(jnp.int32, flipped.shape, 1)
        weight = jnp.sum(jnp.where(lane == z, flipped, 0.0), axis=1, keepdims=True)
        rows_grad = (weight * u_all[block].astype(f32)).astype(bf16)
        x_lo, x_hi = x[:, :half], x[:, half:]
        gate_pre = contract(x_lo, w_g[0], 1, 0) + contract(x_hi, w_g[1], 1, 0)
        up_pre = contract(x_lo, w_u[0], 1, 0) + contract(x_hi, w_u[1], 1, 0)
        hidden_grad = contract(rows_grad[:, :half], w_d[0], 1, 1) + contract(
            rows_grad[:, half:], w_d[1], 1, 1
        )
        sig = jax.nn.sigmoid(gate_pre)
        silu = gate_pre * sig
        hidden = (silu * up_pre).astype(bf16)
        gate_grad = (hidden_grad * up_pre * sig * (1.0 + gate_pre * (1.0 - sig))).astype(bf16)
        up_grad = (hidden_grad * silu).astype(bf16)
        for j in range(2):
            back[block, :, j * half : (j + 1) * half] = (
                contract(gate_grad, w_g[j], 1, 1) + contract(up_grad, w_u[j], 1, 1)
            ).astype(bf16)

        def push(chunks):
            for way in range(2):
                first = (z == 0) & (block > z) if way == 0 else (z == n - 1) & (block < z)

                @pl.when(first)
                def _():
                    for chunk in chunks:
                        if chunk >= FLIGHT:
                            back_copy(way, block, chunk - FLIGHT).wait_send()
                        back_copy(way, block, chunk).start()

        third = -(-(CHUNKS - FLIGHT) // 3)
        push(range(FLIGHT))
        acc_g[...] += contract(x, gate_grad, 0, 0)
        push(range(FLIGHT, min(FLIGHT + third, CHUNKS)))
        acc_u[...] += contract(x, up_grad, 0, 0)
        push(range(FLIGHT + third, min(FLIGHT + 2 * third, CHUNKS)))
        acc_d[...] += contract(hidden, rows_grad, 0, 0)
        push(range(FLIGHT + 2 * third, CHUNKS))

    def turn(i, carry):
        step, side = i // 2, i % 2

        @pl.when((side == 0) & (step > 0))
        def _():
            for way in range(2):
                block = z - step if way == 0 else z + step
                there = block >= 0 if way == 0 else block < n

                @pl.when(there)
                def _():
                    for each in block_copies(way, block):
                        each.wait_recv()

                @pl.when(there & can_go[way])
                def _():
                    for each in block_copies(way, block):
                        each.start()

        block = z - step + 2 * step * side

        @pl.when((block >= 0) & (block < n))
        def _():
            work(block)

        return carry

    work(z)
    lax.fori_loop(2, 2 * n, turn, 0)

    def piece_g(dd, ss):
        return pl.ds(pl.multiple_of((dd * 2 + ss) * rows_g, rows_g), rows_g)

    def piece_d(dd, ss):
        return pl.ds(pl.multiple_of((dd * 2 + ss) * rows_d, rows_d), rows_d)

    for dd in range(2):
        sub_gu[0, dd] = acc_g[piece_g(dd, 1 - s), :].astype(bf16)
        sub_gu[1, dd] = acc_u[piece_g(dd, 1 - s), :].astype(bf16)
        sub_d[dd] = acc_d[piece_d(dd, 1 - s), :].astype(bf16)
    to_sub = [
        copy(sub_gu, got_gu, rs_send.at[0], rs_recv.at[0], sub_peer),
        copy(sub_d, got_d, rs_send.at[1], rs_recv.at[1], sub_peer),
    ]
    for each in to_sub:
        each.start()
    for each in to_sub:
        each.wait_recv()

    def pair(acc, rows, got):
        return acc[rows, :].astype(bf16).astype(f32) + got.astype(f32)

    other = 1 - d
    dp_gu[0] = pair(acc_g, piece_g(other, s), got_gu[0, other]).astype(bf16)
    dp_gu[1] = pair(acc_u, piece_g(other, s), got_gu[1, other]).astype(bf16)
    dp_d[...] = pair(acc_d, piece_d(other, s), got_d[other]).astype(bf16)
    to_dp = [
        copy(dp_gu, in_gu, rs_send.at[2], rs_recv.at[2], dp_peer),
        copy(dp_d, in_d, rs_send.at[3], rs_recv.at[3], dp_peer),
    ]
    for each in to_dp:
        each.start()
    gg_ref[...] = pair(acc_g, piece_g(d, s), got_gu[0, d])
    gu_ref[...] = pair(acc_u, piece_g(d, s), got_gu[1, d])
    gd_ref[...] = pair(acc_d, piece_d(d, s), got_d[d])

    for key in range(1, n):
        def beat(time, carry):
            for way in range(2):
                block = key if way == 0 else n - 1 - key
                chunk = time - z if way == 0 else time - (n - 1 - z)
                relay = (z > 0) & (z < block) if way == 0 else (z < n - 1) & (z > block)

                @pl.when(relay & (chunk >= 0) & (chunk < CHUNKS))
                def _():
                    rows = chunk_rows(chunk)
                    hop = back_copy(way, block, chunk)
                    hop.wait_recv()
                    back[block, rows] = (
                        back[block, rows].astype(f32) + landed[way, block, rows].astype(f32)
                    ).astype(bf16)
                    hop.start()

            return carry

        lax.fori_loop(1, CHUNKS + n - 2, beat, 0)

    for chunk in range(CHUNKS):
        rows = pl.ds(chunk * tall, tall)
        for way in range(2):

            @pl.when(z > 0 if way == 0 else z < n - 1)
            def _():
                back_copy(way, z, chunk).wait_recv()
                back[z, rows] = (
                    back[z, rows].astype(f32) + landed[way, z, rows].astype(f32)
                ).astype(bf16)

        tg_ref[rows, :] = back[z, rows]
    for each in to_dp:
        each.wait_recv()
    gg_ref[...] += in_gu[0].astype(f32)
    gu_ref[...] += in_gu[1].astype(f32)
    gd_ref[...] += in_d[...].astype(f32)

    for each in to_sub + to_dp + weight_copies():
        each.wait_send()
    for block in range(n):

        for way in range(2):

            @pl.when(z < block if way == 0 else z > block)
            def _():
                for chunk in range(CHUNKS - FLIGHT, CHUNKS):
                    back_copy(way, block, chunk).wait_send()

            @pl.when((z > 0) & (z < block) if way == 0 else (z < n - 1) & (z > block))
            def _():
                for chunk in range(CHUNKS - FLIGHT):
                    back_copy(way, block, chunk).wait_send()

        for way in range(2):
            mine = z >= block if way == 0 else z <= block

            @pl.when(mine & can_go[way])
            def _():
                for each in block_copies(way, block):
                    each.wait_send()


def fused(tokens, upstream, routes, gates, w_gate, w_up, w_down):
    f32, bf16 = jnp.float32, jnp.bfloat16
    rows, width = tokens.shape
    n = lax.axis_size("expert")
    depth, hid = w_gate.shape[1:]
    lines = -(-n // 8) * 8
    names = jnp.arange(lines, dtype=jnp.int32)[:, None]
    comb = sum(
        jnp.where(routes[:, k][None, :] == names, gates[:, k][None, :], 0.0) for k in range(TOP)
    )
    dma = pltpu.SemaphoreType.DMA
    quarter_g, quarter_d = width // 4, hid // 4
    outs = pl.pallas_call(
        functools.partial(fused_kernel, n),
        out_shape=(
            jax.ShapeDtypeStruct((rows, width), bf16),
            jax.ShapeDtypeStruct((quarter_g, hid), f32),
            jax.ShapeDtypeStruct((quarter_g, hid), f32),
            jax.ShapeDtypeStruct((quarter_d, width), f32),
        ),
        in_specs=[pl.BlockSpec(memory_space=pltpu.VMEM)] * 6,
        out_specs=[pl.BlockSpec(memory_space=pltpu.VMEM)] * 4,
        scratch_shapes=[
            pltpu.VMEM((n, rows, width), bf16),
            pltpu.VMEM((n, rows, width), bf16),
            pltpu.VMEM((n, lines, rows), f32),
            pltpu.VMEM((2, depth, hid), bf16),
            pltpu.VMEM((2, depth, hid), bf16),
            pltpu.VMEM((2, hid, w_down.shape[2]), bf16),
            pltpu.VMEM((n, rows, width), bf16),
            pltpu.VMEM((2, n, rows, width), bf16),
            pltpu.VMEM((width, hid), f32),
            pltpu.VMEM((width, hid), f32),
            pltpu.VMEM((hid, width), f32),
            pltpu.VMEM((2, 2, quarter_g, hid), bf16),
            pltpu.VMEM((2, quarter_d, width), bf16),
            pltpu.VMEM((2, 2, quarter_g, hid), bf16),
            pltpu.VMEM((2, quarter_d, width), bf16),
            pltpu.VMEM((2, quarter_g, hid), bf16),
            pltpu.VMEM((quarter_d, width), bf16),
            pltpu.VMEM((2, quarter_g, hid), bf16),
            pltpu.VMEM((quarter_d, width), bf16),
            dma((2, n, 3)),
            dma((n, 3)),
            dma((3,)),
            dma((3,)),
            dma((n, CHUNKS)),
            dma((2, n, CHUNKS)),
            dma((4,)),
            dma((4,)),
        ],
        compiler_params=pltpu.CompilerParams(
            collective_id=0, has_side_effects=True, vmem_limit_bytes=56 * 1024 * 1024
        ),
    )(tokens, upstream, comb, w_gate[0], w_up[0], w_down[0])
    return (outs[0], outs[1][None], outs[2][None], outs[3][None])


def per_device(*args):
    small = lax.axis_size("expert") <= 2 * TOP and args[4].shape[0] == 1
    if small and lax.axis_size("dp") == 2 and lax.axis_size("sub") == 2:
        return fused(*args)
    return routed(*args)


def solution(mesh):
    in_specs = (
        P(("groups", "expert", "dp", "sub"), None),
        P(("groups", "expert", "dp", "sub"), None),
        P(("groups", "expert", "dp", "sub"), None),
        P(("groups", "expert", "dp", "sub"), None),
        P("expert", "sub", None),
        P("expert", "sub", None),
        P("expert", None, "sub"),
    )
    out_specs = (
        P(("groups", "expert", "dp", "sub"), None),
        P(("groups", "expert"), ("dp", "sub"), None),
        P(("groups", "expert"), ("dp", "sub"), None),
        P(("groups", "expert"), ("dp", "sub"), None),
    )
    return jax.shard_map(
        per_device, mesh=mesh, in_specs=in_specs, out_specs=out_specs, check_vma=False
    )
```

```python
import functools

import jax
import jax.numpy as jnp
from jax import lax
from jax.experimental import pallas as pl
from jax.experimental.pallas import tpu as pltpu
from jax.sharding import PartitionSpec as P

TOP = 2


def contract(left, right, left_dim, right_dim):
    return lax.dot_general(
        left, right, (((left_dim,), (right_dim,)), ((), ())), preferred_element_type=jnp.float32
    )


def expert_backward(gate_pre, up_pre, rows_grad, gate_mat, up_mat, down_mat):
    sigmoid_gate = jax.nn.sigmoid(gate_pre)
    silu_gate = gate_pre * sigmoid_gate
    hidden = (silu_gate * up_pre).astype(jnp.bfloat16)
    hidden_grad = contract(rows_grad, down_mat, 1, 1)
    gate_grad = (
        hidden_grad * up_pre * sigmoid_gate * (1.0 + gate_pre * (1.0 - sigmoid_gate))
    ).astype(jnp.bfloat16)
    up_grad = (hidden_grad * silu_gate).astype(jnp.bfloat16)
    input_grad = (contract(gate_grad, gate_mat, 1, 1) + contract(up_grad, up_mat, 1, 1)).astype(
        jnp.bfloat16
    )
    return (hidden, gate_grad, up_grad, input_grad)


def routed(tokens, upstream, routes, gates, w_gate, w_up, w_down):
    tok_rows, width = tokens.shape
    experts = lax.axis_size("expert") * w_gate.shape[0]
    capacity = min(tok_rows, 3 * tok_rows * TOP // (2 * experts))
    flat_routes = routes.reshape(-1)
    onehot = (flat_routes[:, None] == jnp.arange(experts, dtype=jnp.int32)[None, :]).astype(
        jnp.int32
    )
    position = jnp.sum((jnp.cumsum(onehot, axis=0) - 1) * onehot, axis=1)
    target = flat_routes * capacity + position
    scaled = (
        (gates[:, :, None] * upstream[:, None, :].astype(jnp.float32))
        .astype(jnp.bfloat16)
        .reshape(-1, width)
    )
    repeated = jnp.repeat(tokens, TOP, axis=0)
    empty_rows = jnp.zeros((experts * capacity, width), jnp.bfloat16)
    send_inputs = empty_rows.at[target].set(repeated).reshape(experts, capacity, width)
    send_grads = empty_rows.at[target].set(scaled).reshape(experts, capacity, width)
    whole = (
        lax.all_gather(w_gate, "sub", axis=1, tiled=True),
        lax.all_gather(w_up, "sub", axis=1, tiled=True),
        lax.all_gather(w_down, "sub", axis=2, tiled=True),
    )
    gate_mat, up_mat, down_mat = (whole[0][0], whole[1][0], whole[2][0])
    got_inputs, got_grads = (
        lax.all_to_all(send_inputs, "expert", split_axis=0, concat_axis=0, tiled=True),
        lax.all_to_all(send_grads, "expert", split_axis=0, concat_axis=0, tiled=True),
    )
    rows_in = got_inputs.reshape(-1, width)
    gate_pre = jnp.dot(rows_in, gate_mat, preferred_element_type=jnp.float32)
    up_pre = jnp.dot(rows_in, up_mat, preferred_element_type=jnp.float32)
    rows_grad = got_grads.reshape(-1, width)
    hidden, gate_grad, up_grad, input_grad = expert_backward(
        gate_pre, up_pre, rows_grad, gate_mat, up_mat, down_mat
    )
    returned = lax.all_to_all(
        input_grad.reshape(experts, capacity, width),
        "expert",
        split_axis=0,
        concat_axis=0,
        tiled=True,
    )
    picked = returned.reshape(-1, width)[target].reshape(tok_rows, TOP, width)
    tokens_grad = jnp.sum(picked.astype(jnp.float32), axis=1).astype(jnp.bfloat16)
    part_gate = contract(rows_in, gate_grad, 0, 0)
    part_up = contract(rows_in, up_grad, 0, 0)
    part_down = contract(hidden, rows_grad, 0, 0)
    summed = (
        lax.psum(part_gate.astype(jnp.bfloat16), ("dp", "sub")).astype(jnp.float32),
        lax.psum(part_up.astype(jnp.bfloat16), ("dp", "sub")).astype(jnp.float32),
        lax.psum(part_down.astype(jnp.bfloat16), ("dp", "sub")).astype(jnp.float32),
    )
    pieces = lax.axis_size(("dp", "sub"))
    member = lax.axis_index(("dp", "sub"))
    slices = [
        lax.dynamic_slice_in_dim(
            matrix, member * (matrix.shape[0] // pieces), matrix.shape[0] // pieces, 0
        )
        for matrix in summed
    ]
    return (tokens_grad, slices[0][None], slices[1][None], slices[2][None])

MESH = pl.DeviceIdType.MESH
CHUNKS = 4
FLIGHT = 4


def fused_kernel(
    n,
    cap,
    tok_ref,
    ups_ref,
    comb_ref,
    wg_ref,
    wu_ref,
    wd_ref,
    tg_ref,
    gg_ref,
    gu_ref,
    gd_ref,
    x_all,
    u_all,
    c_all,
    w_g,
    w_u,
    w_d,
    pack_x,
    pack_u,
    back,
    landed,
    acc_g,
    acc_u,
    acc_d,
    sub_gu,
    sub_d,
    got_gu,
    got_d,
    dp_gu,
    dp_d,
    in_gu,
    in_d,
    ag_send,
    ag_recv,
    w_send,
    w_recv,
    ig_send,
    ig_recv,
    rs_send,
    rs_recv,
):
    f32, bf16 = jnp.float32, jnp.bfloat16
    group = lax.axis_index("groups")
    z = lax.axis_index("expert")
    d = lax.axis_index("dp")
    s = lax.axis_index("sub")
    rows_g = acc_g.shape[0] // 4
    rows_d = acc_d.shape[0] // 4
    half = w_d.shape[2]

    def along(position):
        return (group, position, d, s)

    sub_peer = (group, z, d, 1 - s)
    dp_peer = (group, z, 1 - d, s)

    tail = (n, x_all.shape[1] - cap, x_all.shape[2])
    x_all[:, cap:, :] = jnp.zeros(tail, bf16)
    u_all[:, cap:, :] = jnp.zeros(tail, bf16)
    barrier = pltpu.get_barrier_semaphore()
    for step in range(1, n):
        pl.semaphore_signal(
            barrier, inc=1, device_id=along(lax.rem(z + step, n)), device_id_type=MESH
        )
    pl.semaphore_signal(barrier, inc=1, device_id=sub_peer, device_id_type=MESH)
    pl.semaphore_signal(barrier, inc=1, device_id=dp_peer, device_id_type=MESH)
    x_all[z] = tok_ref[...]
    u_all[z] = ups_ref[...]
    c_all[z] = comb_ref[...]
    w_g[s] = wg_ref[...]
    w_u[s] = wu_ref[...]
    w_d[s] = wd_ref[...]
    pl.semaphore_wait(barrier, n + 1)

    def copy(src, dst, send, recv, peer):
        return pltpu.make_async_remote_copy(
            src_ref=src,
            dst_ref=dst,
            send_sem=send,
            recv_sem=recv,
            device_id=peer,
            device_id_type=MESH,
        )

    size = x_all.shape[1]

    def placing(block, expert, compact):
        comb = c_all[block]
        before = lax.broadcasted_iota(jnp.int32, (size, size), 0)
        after = lax.broadcasted_iota(jnp.int32, (size, size), 1)
        upper = jnp.where(before <= after, 1.0, 0.0).astype(bf16)
        count = contract(jnp.where(comb > 0.0, 1.0, 0.0).astype(bf16), upper, 1, 0)
        line = lax.broadcasted_iota(jnp.int32, comb.shape, 0)
        weight = jnp.sum(jnp.where(line == expert, comb, 0.0), axis=0, keepdims=True)
        count = jnp.sum(jnp.where(line == expert, count, 0.0), axis=0, keepdims=True)
        place = compact * (count - 1.0) + (1.0 - compact) * after[:1].astype(f32)
        hit = (before.astype(f32) == place) & (weight > 0.0)
        column = jnp.sum(jnp.where(hit, weight, 0.0), axis=1, keepdims=True)
        return jnp.where(hit, 1.0, 0.0).astype(bf16), column

    def block_copies(way, block, packed):
        target = jnp.minimum(z + 1, n - 1) if way == 0 else jnp.maximum(z - 1, 0)
        refs = [(c_all.at[block], c_all.at[block])]
        for pack, ref in ((pack_u, u_all), (pack_x, x_all)):
            if packed:
                refs.append((pack.at[way, block], ref.at[block, pl.ds(0, cap)]))
            else:
                refs.append((ref.at[block], ref.at[block]))
        return [
            copy(src, dst, ag_send.at[way, block, i], ag_recv.at[block, i], along(target))
            for i, (src, dst) in enumerate(refs)
        ]

    can_go = (z < n - 1, z > 0)
    to_end = (z == n - 2, z == 1)
    at_end = (z == n - 1, z == 0)

    def send_block(way, block, allowed):
        @pl.when(allowed & jnp.logical_not(to_end[way]))
        def _():
            for each in block_copies(way, block, False):
                each.start()

        @pl.when(allowed & to_end[way])
        def _():
            one_hot = placing(block, n - 1 if way == 0 else 0, 1.0)[0][:cap]
            copies = block_copies(way, block, True)
            copies[0].start()
            pack_u[way, block] = contract(one_hot, u_all[block], 1, 0).astype(bf16)
            copies[1].start()
            pack_x[way, block] = contract(one_hot, x_all[block], 1, 0).astype(bf16)
            copies[2].start()

    for way in range(2):
        send_block(way, z, can_go[way])

    def weight_copies():
        return [
            copy(ref.at[s], ref.at[s], w_send.at[i], w_recv.at[i], sub_peer)
            for i, ref in enumerate((w_g, w_u, w_d))
        ]

    def weight_waits():
        return [
            copy(ref.at[1 - s], ref.at[1 - s], w_send.at[i], w_recv.at[i], sub_peer)
            for i, ref in enumerate((w_g, w_u, w_d))
        ]

    for each in weight_copies():
        each.start()
    acc_g[...] = jnp.zeros_like(acc_g)
    acc_u[...] = jnp.zeros_like(acc_u)
    acc_d[...] = jnp.zeros_like(acc_d)
    for each in weight_waits():
        each.wait_recv()

    tall = back.shape[1] // CHUNKS

    def chunk_rows(chunk):
        return pl.ds(pl.multiple_of(chunk * tall, tall), tall)

    def back_copy(way, block, chunk):
        rows = chunk_rows(chunk)
        target = jnp.minimum(z + 1, n - 1) if way == 0 else jnp.maximum(z - 1, 0)
        return copy(
            back.at[block, rows],
            landed.at[way, block, rows],
            ig_send.at[block, chunk],
            ig_recv.at[way, block, chunk],
            along(target),
        )

    def work(block):
        x = x_all[block]
        ends = (z == 0) | (z == n - 1)
        one_hot, weight = placing(block, z, jnp.where(ends & (block != z), 1.0, 0.0))
        rows_grad = (weight * u_all[block].astype(f32)).astype(bf16)
        x_lo, x_hi = x[:, :half], x[:, half:]
        gate_pre = contract(x_lo, w_g[0], 1, 0) + contract(x_hi, w_g[1], 1, 0)
        up_pre = contract(x_lo, w_u[0], 1, 0) + contract(x_hi, w_u[1], 1, 0)
        hidden_grad = contract(rows_grad[:, :half], w_d[0], 1, 1) + contract(
            rows_grad[:, half:], w_d[1], 1, 1
        )
        sig = jax.nn.sigmoid(gate_pre)
        silu = gate_pre * sig
        hidden = (silu * up_pre).astype(bf16)
        gate_grad = (hidden_grad * up_pre * sig * (1.0 + gate_pre * (1.0 - sig))).astype(bf16)
        up_grad = (hidden_grad * silu).astype(bf16)
        for j in range(2):
            part = contract(gate_grad, w_g[j], 1, 1) + contract(up_grad, w_u[j], 1, 1)
            back[block, :, j * half : (j + 1) * half] = contract(
                one_hot, part.astype(bf16), 0, 0
            ).astype(bf16)

        def push(chunks):
            for way in range(2):
                first = (z == 0) & (block > z) if way == 0 else (z == n - 1) & (block < z)

                @pl.when(first)
                def _():
                    for chunk in chunks:
                        if chunk >= FLIGHT:
                            back_copy(way, block, chunk - FLIGHT).wait_send()
                        back_copy(way, block, chunk).start()

        third = -(-(CHUNKS - FLIGHT) // 3)
        push(range(FLIGHT))
        acc_g[...] += contract(x, gate_grad, 0, 0)
        push(range(FLIGHT, min(FLIGHT + third, CHUNKS)))
        acc_u[...] += contract(x, up_grad, 0, 0)
        push(range(FLIGHT + third, min(FLIGHT + 2 * third, CHUNKS)))
        acc_d[...] += contract(hidden, rows_grad, 0, 0)
        push(range(FLIGHT + 2 * third, CHUNKS))

    def turn(i, carry):
        step, side = i // 2, i % 2

        @pl.when((side == 0) & (step > 0))
        def _():
            for way in range(2):
                block = z - step if way == 0 else z + step
                there = block >= 0 if way == 0 else block < n

                for packed in range(2):
                    form = at_end[way] if packed else jnp.logical_not(at_end[way])

                    @pl.when(there & form)
                    def _():
                        for each in block_copies(way, block, packed):
                            each.wait_recv()

                send_block(way, block, there & can_go[way])

        block = z - step + 2 * step * side

        @pl.when((block >= 0) & (block < n))
        def _():
            work(block)

        return carry

    work(z)
    lax.fori_loop(2, 2 * n, turn, 0)

    def piece_g(dd, ss):
        return pl.ds(pl.multiple_of((dd * 2 + ss) * rows_g, rows_g), rows_g)

    def piece_d(dd, ss):
        return pl.ds(pl.multiple_of((dd * 2 + ss) * rows_d, rows_d), rows_d)

    for dd in range(2):
        sub_gu[0, dd] = acc_g[piece_g(dd, 1 - s), :].astype(bf16)
        sub_gu[1, dd] = acc_u[piece_g(dd, 1 - s), :].astype(bf16)
        sub_d[dd] = acc_d[piece_d(dd, 1 - s), :].astype(bf16)
    to_sub = [
        copy(sub_gu, got_gu, rs_send.at[0], rs_recv.at[0], sub_peer),
        copy(sub_d, got_d, rs_send.at[1], rs_recv.at[1], sub_peer),
    ]
    for each in to_sub:
        each.start()
    for each in to_sub:
        each.wait_recv()

    def pair(acc, rows, got):
        return acc[rows, :].astype(bf16).astype(f32) + got.astype(f32)

    other = 1 - d
    dp_gu[0] = pair(acc_g, piece_g(other, s), got_gu[0, other]).astype(bf16)
    dp_gu[1] = pair(acc_u, piece_g(other, s), got_gu[1, other]).astype(bf16)
    dp_d[...] = pair(acc_d, piece_d(other, s), got_d[other]).astype(bf16)
    to_dp = [
        copy(dp_gu, in_gu, rs_send.at[2], rs_recv.at[2], dp_peer),
        copy(dp_d, in_d, rs_send.at[3], rs_recv.at[3], dp_peer),
    ]
    for each in to_dp:
        each.start()
    gg_ref[...] = pair(acc_g, piece_g(d, s), got_gu[0, d])
    gu_ref[...] = pair(acc_u, piece_g(d, s), got_gu[1, d])
    gd_ref[...] = pair(acc_d, piece_d(d, s), got_d[d])

    for key in range(1, n):
        def beat(time, carry):
            for way in range(2):
                block = key if way == 0 else n - 1 - key
                chunk = time - z if way == 0 else time - (n - 1 - z)
                relay = (z > 0) & (z < block) if way == 0 else (z < n - 1) & (z > block)

                @pl.when(relay & (chunk >= 0) & (chunk < CHUNKS))
                def _():
                    rows = chunk_rows(chunk)
                    hop = back_copy(way, block, chunk)
                    hop.wait_recv()
                    back[block, rows] = (
                        back[block, rows].astype(f32) + landed[way, block, rows].astype(f32)
                    ).astype(bf16)
                    hop.start()

            return carry

        lax.fori_loop(1, CHUNKS + n - 2, beat, 0)

    for chunk in range(CHUNKS):
        rows = pl.ds(chunk * tall, tall)
        for way in range(2):

            @pl.when(z > 0 if way == 0 else z < n - 1)
            def _():
                back_copy(way, z, chunk).wait_recv()
                back[z, rows] = (
                    back[z, rows].astype(f32) + landed[way, z, rows].astype(f32)
                ).astype(bf16)

        tg_ref[rows, :] = back[z, rows]
    for each in to_dp:
        each.wait_recv()
    gg_ref[...] += in_gu[0].astype(f32)
    gu_ref[...] += in_gu[1].astype(f32)
    gd_ref[...] += in_d[...].astype(f32)

    for each in to_sub + to_dp + weight_copies():
        each.wait_send()
    for block in range(n):

        for way in range(2):

            @pl.when(z < block if way == 0 else z > block)
            def _():
                for chunk in range(CHUNKS - FLIGHT, CHUNKS):
                    back_copy(way, block, chunk).wait_send()

            @pl.when((z > 0) & (z < block) if way == 0 else (z < n - 1) & (z > block))
            def _():
                for chunk in range(CHUNKS - FLIGHT):
                    back_copy(way, block, chunk).wait_send()

        for way in range(2):
            mine = z >= block if way == 0 else z <= block

            for packed in range(2):
                form = to_end[way] if packed else jnp.logical_not(to_end[way])

                @pl.when(mine & can_go[way] & form)
                def _():
                    for each in block_copies(way, block, packed):
                        each.wait_send()


def fused(tokens, upstream, routes, gates, w_gate, w_up, w_down):
    f32, bf16 = jnp.float32, jnp.bfloat16
    rows, width = tokens.shape
    n = lax.axis_size("expert")
    depth, hid = w_gate.shape[1:]
    lines = -(-n // 8) * 8
    cap = min(rows, 3 * rows * TOP // (2 * n))
    names = jnp.arange(lines, dtype=jnp.int32)[:, None]
    comb = sum(
        jnp.where(routes[:, k][None, :] == names, gates[:, k][None, :], 0.0) for k in range(TOP)
    )
    dma = pltpu.SemaphoreType.DMA
    quarter_g, quarter_d = width // 4, hid // 4
    outs = pl.pallas_call(
        functools.partial(fused_kernel, n, cap),
        out_shape=(
            jax.ShapeDtypeStruct((rows, width), bf16),
            jax.ShapeDtypeStruct((quarter_g, hid), f32),
            jax.ShapeDtypeStruct((quarter_g, hid), f32),
            jax.ShapeDtypeStruct((quarter_d, width), f32),
        ),
        in_specs=[pl.BlockSpec(memory_space=pltpu.VMEM)] * 6,
        out_specs=[pl.BlockSpec(memory_space=pltpu.VMEM)] * 4,
        scratch_shapes=[
            pltpu.VMEM((n, rows, width), bf16),
            pltpu.VMEM((n, rows, width), bf16),
            pltpu.VMEM((n, lines, rows), f32),
            pltpu.VMEM((2, depth, hid), bf16),
            pltpu.VMEM((2, depth, hid), bf16),
            pltpu.VMEM((2, hid, w_down.shape[2]), bf16),
            pltpu.VMEM((2, n, cap, width), bf16),
            pltpu.VMEM((2, n, cap, width), bf16),
            pltpu.VMEM((n, rows, width), bf16),
            pltpu.VMEM((2, n, rows, width), bf16),
            pltpu.VMEM((width, hid), f32),
            pltpu.VMEM((width, hid), f32),
            pltpu.VMEM((hid, width), f32),
            pltpu.VMEM((2, 2, quarter_g, hid), bf16),
            pltpu.VMEM((2, quarter_d, width), bf16),
            pltpu.VMEM((2, 2, quarter_g, hid), bf16),
            pltpu.VMEM((2, quarter_d, width), bf16),
            pltpu.VMEM((2, quarter_g, hid), bf16),
            pltpu.VMEM((quarter_d, width), bf16),
            pltpu.VMEM((2, quarter_g, hid), bf16),
            pltpu.VMEM((quarter_d, width), bf16),
            dma((2, n, 3)),
            dma((n, 3)),
            dma((3,)),
            dma((3,)),
            dma((n, CHUNKS)),
            dma((2, n, CHUNKS)),
            dma((4,)),
            dma((4,)),
        ],
        compiler_params=pltpu.CompilerParams(
            collective_id=0, has_side_effects=True, vmem_limit_bytes=56 * 1024 * 1024
        ),
    )(tokens, upstream, comb, w_gate[0], w_up[0], w_down[0])
    return (outs[0], outs[1][None], outs[2][None], outs[3][None])


def per_device(*args):
    small = lax.axis_size("expert") <= 2 * TOP and args[4].shape[0] == 1
    if small and lax.axis_size("dp") == 2 and lax.axis_size("sub") == 2:
        return fused(*args)
    return routed(*args)


def solution(mesh):
    in_specs = (
        P(("groups", "expert", "dp", "sub"), None),
        P(("groups", "expert", "dp", "sub"), None),
        P(("groups", "expert", "dp", "sub"), None),
        P(("groups", "expert", "dp", "sub"), None),
        P("expert", "sub", None),
        P("expert", "sub", None),
        P("expert", None, "sub"),
    )
    out_specs = (
        P(("groups", "expert", "dp", "sub"), None),
        P(("groups", "expert"), ("dp", "sub"), None),
        P(("groups", "expert"), ("dp", "sub"), None),
        P(("groups", "expert"), ("dp", "sub"), None),
    )
    return jax.shard_map(
        per_device, mesh=mesh, in_specs=in_specs, out_specs=out_specs, check_vma=False
    )
```
